32 devices in a mesh: segment: 2 (over x), win: 4 (over y, core), head: 4 (over z).
Axes of the slice: x: 2, y: 2, z: 4, core: 2. Of those that a mesh axis runs over, the one named last changes fastest.
Arguments:
- inputs: bfloat16 [2, 30, 120, 1536], P(None, None, 'win', 'head'), may hold values from -16 to 16
- gains: float32 [2, 1536], P('segment'), may hold values from 0.1 to 1.9
- qkv_weight: bfloat16 [2, 1536, 3, 1536], P('segment', None, None, 'head'), may hold values from -3.5 to 3.5
- out_weight: bfloat16 [2, 1536, 1536], P('segment', 'head'), may hold values from -0.15625 to 0.15625
- labels: int32 [30, 120], P(None, 'win'), may hold values from 0 to 3, as said below
Outputs:
- sections: bfloat16 [2, 2, 30, 120, 1536], P('segment', None, None, 'win', 'head')
The draws below stay inside these ranges and needn't reach their ends.
Inputs may be any that keep to these rules, and one draw needn't show every extreme that they name: In each window of 30 by 30 cells the label is 2 on the rows from a drawn row cut on plus 1 on the columns from a drawn column cut on; both cuts lie in 1 to 29, so every window holds all four labels.
All inputs are finite; a program needn't handle non-finite values.
Results may differ from the reference program's by a relative error of at most 0.013.
Values may be sent and summed in bfloat16 or wider, within the bound.
A program may use at most 128 MiB of HBM per device.

```python
import math
import jax
import jax.numpy as jnp
from jax import lax

D = 1536
HEADS = 12
HEAD_DIM = 128
WIN_SIDE = 30
MB = 2
COLS = 120
N_SEGMENT = 2


def draw_inputs(key, part):
    subkeys = jax.random.split(key, 3)
    full_shape = (MB, WIN_SIDE, COLS, D)
    draws_base = jax.random.normal(subkeys[0], full_shape, jnp.float32)
    row_scale = jnp.exp(jax.random.uniform(subkeys[1], (MB, WIN_SIDE, COLS, 1), jnp.float32, -1.15, 1.15))
    col_scale = jnp.exp(jax.random.uniform(subkeys[2], (D,), jnp.float32, -1.15, 1.15))
    values = draws_base * row_scale * col_scale
    return jnp.clip(values, -16.0, 16.0).astype(jnp.bfloat16)


def draw_qkv_weight(key, part):
    subkeys = jax.random.split(key, 1)
    full_shape = (2, D, 3, D)
    raw_draw = jnp.clip(jax.random.normal(subkeys[0], full_shape, jnp.float32), -6.0, 6.0) / math.sqrt(D)
    slot_gain = jnp.array([1.6, 1.6, 2.0], jnp.float32)[None, None, :, None]
    weights_drawn = raw_draw * slot_gain
    return jnp.clip(weights_drawn, -3.5, 3.5).astype(jnp.bfloat16)


def draw_labels(key, part):
    subkeys = jax.random.split(key, 2)
    win_count = COLS // WIN_SIDE
    row_cut = jax.random.randint(subkeys[0], (win_count,), 1, WIN_SIDE)
    col_cut = jax.random.randint(subkeys[1], (win_count,), 1, WIN_SIDE)
    row_pos = jnp.arange(WIN_SIDE)[:, None]
    col_pos = jnp.arange(COLS)[None, :]
    owner = col_pos // WIN_SIDE
    inner = col_pos % WIN_SIDE
    lower = (row_pos >= row_cut[owner]).astype(jnp.int32)
    right = (inner >= col_cut[owner]).astype(jnp.int32)
    return (2 * lower + right).astype(jnp.int32)


def level_of(rng, shape, cuts, smallest, high):
    loudness = 1.0
    for axis_at, shards_of in cuts:
        draws = jax.random.uniform(jax.random.fold_in(jax.random.fold_in(rng, 6), axis_at), (shards_of,), jnp.float32, smallest / len(cuts), high / len(cuts))
        loudness = loudness * jnp.repeat(jnp.exp(draws), shape[axis_at] // shards_of).reshape((-1,) + (1,) * (len(shape) - 1 - axis_at))
    return loudness


def normal_values(own_key, extent, deviation, most, pieces=(), held_as=jnp.bfloat16):
    factor_of = level_of(own_key, extent, pieces, -0.22, 0.18) if pieces else 1.0
    values = jax.random.normal(own_key, extent, jnp.float32) * deviation * factor_of
    return jnp.minimum(jnp.maximum(values, -most), most).astype(held_as)


def setup_inputs(seed: int = 0) -> dict:
    splits = jax.random.split(jax.random.key(seed), 6)
    return {
        "inputs": draw_inputs(jax.random.fold_in(splits[5], 71), 0),
        "gains": jnp.clip(1.0 + 0.18 * jax.random.normal(splits[1], (N_SEGMENT, D), jnp.float32), 0.1, 1.9),
        "qkv_weight": draw_qkv_weight(jax.random.fold_in(splits[5], 71), 0),
        "out_weight": normal_values(splits[3], (N_SEGMENT, D, D), D ** -0.5, 0.15625, ((0, 2), (1, 4))),
        "labels": draw_labels(jax.random.fold_in(splits[5], 71), 0),
    }


def rms_normed(slab, gain_row):
    values_f = slab.astype(jnp.float32)
    mean_square = lax.optimization_barrier(jnp.mean(values_f * values_f, axis=-1, keepdims=True))
    return (values_f * lax.rsqrt(mean_square + 1e-05) * gain_row).astype(jnp.bfloat16)

def to_windows(grid):
    win_rows = grid.shape[0]
    win_count = grid.shape[1] // win_rows
    features = grid.shape[2]
    return grid.reshape(win_rows, win_count, win_rows, features).transpose(1, 0, 2, 3).reshape(win_count, win_rows * win_rows, features)

def from_windows(blocks, win_rows):
    win_count = blocks.shape[0]
    features = blocks.shape[2]
    return blocks.reshape(win_count, win_rows, win_rows, features).transpose(1, 0, 2, 3).reshape(win_rows, win_count * win_rows, features)

def section_layer(slab, gain_row, wqkv, wout, labels, use_labels):
    normed = rms_normed(slab, gain_row)
    win_normed = to_windows(normed)
    win_labels = to_windows(labels[:, :, None])[:, :, 0]
    flat_qkv = wqkv.reshape(D, 3 * D)

    def one_window(pair):
        normed_win, labels_win = pair
        qkv_all = jnp.dot(normed_win, flat_qkv, preferred_element_type=jnp.float32).astype(jnp.bfloat16)
        qkv_all = qkv_all.reshape(-1, 3, HEADS, HEAD_DIM).astype(jnp.float32)
        queries = qkv_all[:, 0]
        keys_all = qkv_all[:, 1]
        values_all = qkv_all[:, 2]
        scores = jnp.einsum('qhe,khe->hqk', queries, keys_all) * HEAD_DIM ** (-0.5)
        if use_labels:
            allowed = labels_win[:, None] == labels_win[None, :]
            scores = jnp.where(allowed[None], scores, -1e+30)
        top_score = lax.optimization_barrier(jnp.max(scores, axis=-1, keepdims=True))
        expo = jnp.exp(scores - top_score)
        attn_prob = (expo / lax.optimization_barrier(jnp.sum(expo, axis=-1, keepdims=True))).astype(jnp.bfloat16)
        attended = jnp.einsum('hqk,khe->qhe', attn_prob.astype(jnp.float32), values_all).astype(jnp.bfloat16)
        attended = attended.reshape(-1, D)
        return jnp.dot(attended, wout, preferred_element_type=jnp.float32)
    projected = lax.map(one_window, (win_normed, win_labels))
    projected = from_windows(projected, WIN_SIDE)
    return (slab.astype(jnp.float32) + projected).astype(jnp.bfloat16)

def reference(inputs, gains, qkv_weight, out_weight, labels):
    half_cols = WIN_SIDE // 2
    firsts = []
    seconds = []
    for micro in range(MB):
        first = section_layer(inputs[micro], gains[0], qkv_weight[0], out_weight[0], labels, False)
        shifted = jnp.roll(first, -half_cols, axis=1)
        second = section_layer(shifted, gains[1], qkv_weight[1], out_weight[1], labels, True)
        firsts.append(first)
        seconds.append(second)
    return jnp.stack([jnp.stack(firsts), jnp.stack(seconds)])
```

```python
import functools
import math

import jax
import jax.numpy as jnp
from jax import lax
from jax.experimental import pallas as pl
from jax.experimental.pallas import tpu as pltpu
from jax.sharding import PartitionSpec as P

HEAD_DIM = 128
WIN_SIDE = 30
MESH = pl.DeviceIdType.MESH
LAYERS = 2


def pad16(n):
    return -(-n // 16) * 16


def remote(src, dst, send, recv, device):
    return pltpu.make_async_remote_copy(
        src_ref=src, dst_ref=dst, send_sem=send, recv_sem=recv,
        device_id=device, device_id_type=MESH,
    )


def two_layers(
    n_head, n_win, half,
    x_ref, gain_ref, lq_ref, lk_ref, wq_hbm, wo_hbm,
    out_ref,
    wq, wo, gb, ag, normed, qkv, vx, attb, part, parts_in, own, cur, first_a, second,
    loc_sem, wsend, wrecv, fsend, frecv, ag_send, ag_recv, rs_send, rs_recv,
    roll_send, roll_recv, o_send, o_recv,
):
    seg = lax.axis_index("segment")
    win = lax.axis_index("win")
    me = lax.axis_index("head")
    other = 1 - seg
    core = lax.rem(win, 2)
    mate = win + 1 - 2 * core
    left = lax.rem(win + n_win - 1, n_win)
    right = lax.rem(win + 1, n_win)
    peers = [lax.rem(me + d, n_head) for d in range(1, n_head)]
    tokens, feat = x_ref.shape
    heads = feat // HEAD_DIM
    first_rows = pad16(half // 2)
    subs = ((0, first_rows), (first_rows, half - first_rows))

    barrier = pltpu.get_barrier_semaphore()
    for peer in peers:
        pl.semaphore_signal(barrier, inc=1, device_id={"head": peer}, device_id_type=MESH)
    pl.semaphore_signal(barrier, inc=1, device_id={"segment": other}, device_id_type=MESH)
    for w in (mate, left, right):
        pl.semaphore_signal(barrier, inc=1, device_id={"win": w}, device_id_type=MESH)

    wq_local = pltpu.make_async_copy(wq_hbm, wq.at[seg], loc_sem.at[0])
    wo_local = pltpu.make_async_copy(wo_hbm, wo.at[seg], loc_sem.at[1])
    wq_local.start()
    wo_local.start()
    pl.semaphore_wait(barrier, n_head - 1 + 4)

    def gather_copies(layer, h, src):
        rows = pl.ds(h * half, half)
        return [
            remote(src.at[rows], ag.at[layer, d, rows], ag_send.at[layer, h, d],
                   ag_recv.at[layer, h, d], {"head": peers[d]})
            for d in range(n_head - 1)
        ]

    gathers = [[None, None], [None, None]]
    for h in range(2):
        gathers[0][h] = gather_copies(0, h, x_ref)
        for c in gathers[0][h]:
            c.start()

    q_rows, o_rows = wq_hbm.shape[0] // 2, wo_hbm.shape[0] // 2
    mine_q = pl.ds(pl.multiple_of(core * q_rows, 16), q_rows)
    mine_o = pl.ds(pl.multiple_of(core * o_rows, 16), o_rows)
    mate_q = pl.ds(pl.multiple_of((1 - core) * q_rows, 16), q_rows)
    mate_o = pl.ds(pl.multiple_of((1 - core) * o_rows, 16), o_rows)
    there, beside = {"segment": other}, {"win": mate}
    gain_out = remote(gain_ref, gb.at[seg], wsend.at[2], wrecv.at[2], there)
    wq_out = remote(wq_hbm.at[mine_q], wq.at[seg, mine_q], wsend.at[0], wrecv.at[0], there)
    wo_out = remote(wo_hbm.at[mine_o], wo.at[seg, mine_o], wsend.at[1], wrecv.at[1], there)
    gain_out.start()
    wq_out.start()
    wo_out.start()
    gb[seg] = gain_ref[...]
    for h in range(heads):
        vx[h, :, HEAD_DIM:] = jnp.ones((tokens, HEAD_DIM), jnp.bfloat16)

    wq_in = remote(wq_hbm.at[mine_q], wq.at[other, mine_q], wsend.at[0], wrecv.at[0], there)
    wo_in = remote(wo_hbm.at[mine_o], wo.at[other, mine_o], wsend.at[1], wrecv.at[1], there)
    gain_in = remote(gain_ref, gb.at[other], wsend.at[2], wrecv.at[2], there)
    wq_fwd = remote(wq.at[other, mine_q], wq.at[other, mine_q], fsend.at[0], frecv.at[0], beside)
    wo_fwd = remote(wo.at[other, mine_o], wo.at[other, mine_o], fsend.at[1], frecv.at[1], beside)
    wq_fwd_in = remote(wq.at[other, mate_q], wq.at[other, mate_q], fsend.at[0], frecv.at[0], beside)
    wo_fwd_in = remote(wo.at[other, mate_o], wo.at[other, mate_o], fsend.at[1], frecv.at[1], beside)

    def part_copy(layer, block, rows, d):
        return remote(part.at[layer, d, rows], parts_in.at[layer, d, rows],
                      rs_send.at[layer, block, d], rs_recv.at[layer, block, d],
                      {"head": peers[d]})

    def columns(owner):
        return pl.ds(pl.multiple_of(owner * feat, 128), feat)

    def layer_compute(layer, src):
        for h in range(2):
            for c in gathers[layer][h]:
                c.wait_recv()

        def norm_half(i, carry):
            rows = pl.ds(pl.multiple_of(i * half, 16), half)

            def chunk(d):
                return (src[rows, :] if d < 0 else ag[layer, d, rows, :]).astype(jnp.float32)

            total = jnp.zeros((half, 1), jnp.float32)
            for d in range(-1, n_head - 1):
                value = chunk(d)
                total = total + jnp.sum(value * value, axis=-1, keepdims=True)
            scale = lax.rsqrt(total / (feat * n_head) + 1e-05)
            for d in range(-1, n_head - 1):
                owner = lax.rem(me + n_head - 1 - d, n_head)
                value = chunk(d) * scale * gb[layer, 0:1, columns(owner)]
                normed[rows, columns(owner)] = value.astype(jnp.bfloat16)
            return carry

        lax.fori_loop(0, 2, norm_half, 0)
        if layer == 0:
            wq_local.wait()
            wq_fwd_in.wait_recv()

        def qkv_half(i, carry):
            rows = pl.ds(pl.multiple_of(i * half, 16), half)
            for slot in range(3):
                cols = slice(slot * feat, (slot + 1) * feat)
                value = jnp.dot(normed[rows, :], wq[layer, :, cols],
                                preferred_element_type=jnp.float32)
                if slot == 0:
                    value = value * (HEAD_DIM ** -0.5 * math.log2(math.e))
                if slot < 2:
                    qkv[rows, cols] = value.astype(jnp.bfloat16)
                else:
                    for h in range(heads):
                        vx[h, rows, :HEAD_DIM] = value[
                            :, h * HEAD_DIM:(h + 1) * HEAD_DIM].astype(jnp.bfloat16)
            return carry

        lax.fori_loop(0, 2, qkv_half, 0)
        if layer == 0:
            wo_in.wait_recv()
            wo_fwd.start()
            wo_local.wait()
            wo_fwd_in.wait_recv()

        def attend_half(i, carry):
            for sub, (offset, count) in enumerate(subs):
                rows = pl.ds(pl.multiple_of(i * half + offset, 16), count)
                for h in range(heads):
                    q = qkv[rows, h * HEAD_DIM:(h + 1) * HEAD_DIM]
                    k = qkv[:, feat + h * HEAD_DIM:feat + (h + 1) * HEAD_DIM]
                    scores = lax.dot_general(q, k, (((1,), (1,)), ((), ())),
                                             preferred_element_type=jnp.float32)
                    scores = jnp.where(lq_ref[layer, rows, :] == lk_ref[layer], scores, -1e30)
                    top = jnp.max(scores, axis=-1, keepdims=True)
                    expo = jnp.exp2(scores - top).astype(jnp.bfloat16)
                    both = jnp.dot(expo, vx[h], preferred_element_type=jnp.float32)
                    attb[rows, h * HEAD_DIM:(h + 1) * HEAD_DIM] = (
                        both[:, :HEAD_DIM] / both[:, HEAD_DIM:]).astype(jnp.bfloat16)
                block = attb[rows, :]
                for d in range(n_head - 1):
                    part[layer, d, rows, :] = jnp.dot(
                        block, wo[layer, :, columns(peers[d])],
                        preferred_element_type=jnp.float32).astype(jnp.bfloat16)
                    part_copy(layer, i * 2 + sub, rows, d).start()
                own[rows, :] = jnp.dot(block, wo[layer, :, columns(me)],
                                       preferred_element_type=jnp.float32)
            return carry

        lax.fori_loop(0, 2, attend_half, 0)

    def finish(layer, src, h, sub):
        offset, count = subs[sub]
        rows = pl.ds(h * half + offset, count)
        total = src[rows, :].astype(jnp.float32) + own[rows, :]
        for d in range(n_head - 1):
            part_copy(layer, h * 2 + sub, rows, d).wait_recv()
            total = total + parts_in[layer, d, rows, :].astype(jnp.float32)
        return rows, total.astype(jnp.bfloat16)

    wq_in.wait_recv()
    wq_fwd.start()
    gain_in.wait_recv()
    layer_compute(0, x_ref)

    low, high = pl.ds(0, half), pl.ds(half, half)
    rolls = []
    for sub, (offset, count) in enumerate(subs):
        rows, value = finish(0, x_ref, 0, sub)
        first_a[rows, :] = value
        roll = remote(first_a.at[rows], cur.at[pl.ds(half + offset, count)],
                      roll_send.at[sub], roll_recv.at[sub], {"win": left})
        roll.start()
        rolls.append(roll)
    for sub, (offset, count) in enumerate(subs):
        rows, value = finish(0, x_ref, 1, sub)
        cur[pl.ds(offset, count), :] = value
    gathers[1][0] = gather_copies(1, 0, cur)
    for c in gathers[1][0]:
        c.start()
    for roll in rolls:
        roll.wait_recv()
    gathers[1][1] = gather_copies(1, 1, cur)
    for c in gathers[1][1]:
        c.start()

    first_out = [
        remote(first_a, out_ref.at[seg, low], o_send.at[0], o_recv.at[0], there),
        remote(cur.at[low], out_ref.at[seg, high], o_send.at[1], o_recv.at[1], there),
    ]
    first_in = [
        remote(first_a, out_ref.at[other, low], o_send.at[0], o_recv.at[0], there),
        remote(cur.at[low], out_ref.at[other, high], o_send.at[1], o_recv.at[1], there),
    ]

    @pl.when(seg == 0)
    def _():
        out_ref[seg, low, :] = first_a[...]
        out_ref[seg, high, :] = cur[low, :]

    @pl.when(seg == 1)
    def _():
        for c in first_out:
            c.start()

    layer_compute(1, cur)

    second_sends, second_recvs = [], []
    for h in range(2):
        for sub in range(2):
            rows, value = finish(1, cur, h, sub)
            block = 2 + h * 2 + sub
            send = remote(second.at[rows], out_ref.at[seg, rows], o_send.at[block],
                          o_recv.at[block], there)
            second_sends.append(send)
            second_recvs.append(remote(second.at[rows], out_ref.at[other, rows],
                                       o_send.at[block], o_recv.at[block], there))
            second[rows, :] = value

            @pl.when(seg == 0)
            def _(send=send):
                send.start()

            @pl.when(seg == 1)
            def _(rows=rows, value=value):
                out_ref[seg, rows, :] = second[rows, :]

    for layer in range(2):
        for h in range(2):
            for c in gathers[layer][h]:
                c.wait_send()
            for sub, (offset, count) in enumerate(subs):
                rows = pl.ds(h * half + offset, count)
                for d in range(n_head - 1):
                    part_copy(layer, h * 2 + sub, rows, d).wait_send()
    for c in (gain_out, wq_out, wo_out, wq_fwd, wo_fwd, *rolls):
        c.wait_send()

    @pl.when(seg == 0)
    def _():
        for c in first_in:
            c.wait_recv()
        for c in second_sends:
            c.wait_send()

    @pl.when(seg == 1)
    def _():
        for c in first_out:
            c.wait_send()
        for c in second_recvs:
            c.wait_recv()


def to_halves(grid, half, fill):
    rows, cols, features = grid.shape
    split = grid.reshape(rows, 2, cols // 2, features).transpose(1, 0, 2, 3)
    split = split.reshape(2, rows * (cols // 2), features)
    split = jnp.pad(split, ((0, 0), (0, half - split.shape[1]), (0, 0)), constant_values=fill)
    return split.reshape(2 * half, features)


def body(n_head, n_win, inputs, gains, qkv_weight, out_weight, labels):
    seg = lax.axis_index("segment")
    micro, win_rows, win_cols, feat = inputs.shape
    cells = win_rows * (win_cols // 2)
    half = pad16(cells)
    tokens = 2 * half
    model = feat * n_head
    heads = feat // HEAD_DIM
    x = lax.dynamic_index_in_dim(inputs, seg, 0, keepdims=False)
    x = to_halves(x, half, 0)
    grid = labels[:, :, None]
    keys = jnp.stack([to_halves(jnp.zeros_like(grid), half, -1), to_halves(grid, half, -1)])
    queries = jnp.maximum(keys, 0)
    keys = keys.reshape(LAYERS, 1, tokens)
    gain_rows = jnp.broadcast_to(gains, (8, model))
    wq = qkv_weight[0].reshape(model, 3 * feat)
    wo = out_weight[0]
    bf16, f32 = jnp.bfloat16, jnp.float32
    others = n_head - 1
    dma = pltpu.SemaphoreType.DMA
    vmem = pl.BlockSpec(memory_space=pltpu.VMEM)
    hbm = pl.BlockSpec(memory_space=pl.ANY)
    out = pl.pallas_call(
        functools.partial(two_layers, n_head, n_win, half),
        out_shape=jax.ShapeDtypeStruct((micro, tokens, feat), bf16),
        in_specs=[vmem, vmem, vmem, vmem, hbm, hbm],
        out_specs=vmem,
        scratch_shapes=[
            pltpu.VMEM((LAYERS, model, 3 * feat), bf16),
            pltpu.VMEM((LAYERS, feat, model), bf16),
            pltpu.VMEM((LAYERS, 8, model), f32),
            pltpu.VMEM((LAYERS, others, tokens, feat), bf16),
            pltpu.VMEM((tokens, model), bf16),
            pltpu.VMEM((tokens, 2 * feat), bf16),
            pltpu.VMEM((heads, tokens, 2 * HEAD_DIM), bf16),
            pltpu.VMEM((tokens, feat), bf16),
            pltpu.VMEM((LAYERS, others, tokens, feat), bf16),
            pltpu.VMEM((LAYERS, others, tokens, feat), bf16),
            pltpu.VMEM((tokens, feat), f32),
            pltpu.VMEM((tokens, feat), bf16),
            pltpu.VMEM((half, feat), bf16),
            pltpu.VMEM((tokens, feat), bf16),
            dma((2,)), dma((3,)), dma((3,)), dma((2,)), dma((2,)),
            dma((LAYERS, 2, others)), dma((LAYERS, 2, others)),
            dma((LAYERS, 4, others)), dma((LAYERS, 4, others)),
            dma((2,)), dma((2,)), dma((6,)), dma((6,)),
        ],
        compiler_params=pltpu.CompilerParams(
            collective_id=0, has_side_effects=True, vmem_limit_bytes=58 * 2 ** 20),
    )(x, gain_rows, queries, keys, wq, wo)
    out = out.reshape(micro, 2, half, feat)[:, :, :cells]
    out = out.reshape(micro, 2, win_rows, win_cols // 2, feat).transpose(0, 2, 1, 3, 4)
    return out.reshape(1, micro, win_rows, win_cols, feat)


def solution(mesh):
    in_specs = (
        P(None, None, "win", "head"),
        P("segment", None),
        P("segment", None, None, "head"),
        P("segment", "head", None),
        P(None, "win"),
    )
    out_specs = P("segment", None, None, "win", "head")
    run = functools.partial(body, mesh.shape["head"], mesh.shape["win"])
    return jax.shard_map(run, mesh=mesh, in_specs=in_specs, out_specs=out_specs, check_vma=False)
```

```python
import functools
import math

import jax
import jax.numpy as jnp
from jax import lax
from jax.experimental import pallas as pl
from jax.experimental.pallas import tpu as pltpu
from jax.sharding import PartitionSpec as P

HEAD_DIM = 128
WIN_SIDE = 30
MESH = pl.DeviceIdType.MESH
LAYERS = 2


def pad16(n):
    return -(-n // 16) * 16


def remote(src, dst, send, recv, device):
    return pltpu.make_async_remote_copy(
        src_ref=src, dst_ref=dst, send_sem=send, recv_sem=recv,
        device_id=device, device_id_type=MESH,
    )


def two_layers(
    n_head, n_win, half,
    x_ref, gain_ref, lq_ref, lk_ref, wq_hbm, wo_hbm,
    out_ref,
    wq, wo, gb, ag, normed, qkv, vx, attb, part, sums, sums_in, cur, first_a, second,
    loc_sem, wsend, wrecv, fsend, frecv, ag_send, ag_recv, rs_send, rs_recv,
    roll_send, roll_recv, o_send, o_recv,
):
    seg = lax.axis_index("segment")
    win = lax.axis_index("win")
    me = lax.axis_index("head")
    last = n_head - 1
    other = 1 - seg
    core = lax.rem(win, 2)
    mate = win + 1 - 2 * core
    left = lax.rem(win + n_win - 1, n_win)
    right = lax.rem(win + 1, n_win)
    tokens, feat = x_ref.shape
    heads = feat // HEAD_DIM
    first_rows = pad16(half // 2)
    blocks = ((0, first_rows), (first_rows, half - first_rows),
              (half, first_rows), (half + first_rows, half - first_rows))
    up, down = {"head": me + 1}, {"head": me - 1}
    there, beside = {"segment": other}, {"win": mate}

    wq_local = pltpu.make_async_copy(wq_hbm, wq.at[seg], loc_sem.at[0])
    wo_local = pltpu.make_async_copy(wo_hbm, wo.at[seg], loc_sem.at[1])
    wq_local.start()
    wo_local.start()

    barrier = pltpu.get_barrier_semaphore()

    @pl.when(me < last)
    def _():
        pl.semaphore_signal(barrier, inc=1, device_id=up, device_id_type=MESH)

    @pl.when(me > 0)
    def _():
        pl.semaphore_signal(barrier, inc=1, device_id=down, device_id_type=MESH)

    pl.semaphore_signal(barrier, inc=1, device_id=there, device_id_type=MESH)
    for w in (mate, left, right):
        pl.semaphore_signal(barrier, inc=1, device_id={"win": w}, device_id_type=MESH)

    @pl.when((me > 0) & (me < last))
    def _():
        pl.semaphore_wait(barrier, 6)

    @pl.when((me == 0) | (me == last))
    def _():
        pl.semaphore_wait(barrier, 5)

    def rows_of(block):
        return pl.ds(blocks[block][0], blocks[block][1])

    def ag_copy(layer, way, hop, block, owner, src):
        rows = rows_of(block)
        source = ag.at[layer, owner, rows] if src is None else src.at[rows]
        return remote(source, ag.at[layer, owner, rows], ag_send.at[layer, way, hop, block],
                      ag_recv.at[layer, way, hop, block], up if way == 0 else down)

    def gather_start(layer, src, block):
        @pl.when(me < last)
        def _():
            ag_copy(layer, 0, 0, block, me, src).start()

        @pl.when(me > 0)
        def _():
            ag_copy(layer, 1, 0, block, me, src).start()

    def gather_step(layer, hop, block):
        behind, ahead = me - 1 - hop, me + 1 + hop

        @pl.when(behind >= 0)
        def _():
            ag_copy(layer, 0, hop, block, behind, None).wait_recv()
            if hop + 1 < last:
                @pl.when(me < last)
                def _():
                    ag_copy(layer, 0, hop + 1, block, behind, None).start()

        @pl.when(ahead <= last)
        def _():
            ag_copy(layer, 1, hop, block, ahead, None).wait_recv()
            if hop + 1 < last:
                @pl.when(me > 0)
                def _():
                    ag_copy(layer, 1, hop + 1, block, ahead, None).start()

    def gather_sent(layer, src, block):
        for hop in range(last):
            @pl.when((me - hop >= 0) & (me < last))
            def _(hop=hop):
                ag_copy(layer, 0, hop, block, me - hop, None if hop else src).wait_send()

            @pl.when((me + hop <= last) & (me > 0))
            def _(hop=hop):
                ag_copy(layer, 1, hop, block, me + hop, None if hop else src).wait_send()

    def sum_copy(layer, way, block, rows, owner):
        return remote(sums.at[layer, owner, rows], sums_in.at[layer, way, owner, rows],
                      rs_send.at[layer, way, block, owner], rs_recv.at[layer, way, block, owner],
                      up if way == 0 else down)

    q_rows, o_rows = wq_hbm.shape[1] // 2, wo_hbm.shape[0] // 2
    mine_q = pl.ds(pl.multiple_of(core * q_rows, 16), q_rows)
    mine_o = pl.ds(pl.multiple_of(core * o_rows, 16), o_rows)
    mate_q = pl.ds(pl.multiple_of((1 - core) * q_rows, 16), q_rows)
    mate_o = pl.ds(pl.multiple_of((1 - core) * o_rows, 16), o_rows)
    every = pl.ds(0, 3)

    for block in range(4):
        gather_start(0, x_ref, block)
    gain_out = remote(gain_ref, gb.at[seg], wsend.at[2], wrecv.at[2], there)
    wq_out = remote(wq_hbm.at[every, mine_q], wq.at[seg, every, mine_q],
                    wsend.at[0], wrecv.at[0], there)
    wo_out = remote(wo_hbm.at[mine_o], wo.at[seg, mine_o], wsend.at[1], wrecv.at[1], there)
    gain_out.start()
    wq_out.start()
    wo_out.start()
    gb[seg] = gain_ref[...]
    for h in range(heads):
        vx[h, :, HEAD_DIM:] = jnp.ones((tokens, HEAD_DIM), jnp.bfloat16)

    wq_theirs, wq_mates = wq.at[other, every, mine_q], wq.at[other, every, mate_q]
    wq_in = remote(wq_hbm.at[every, mine_q], wq_theirs, wsend.at[0], wrecv.at[0], there)
    wo_in = remote(wo_hbm.at[mine_o], wo.at[other, mine_o], wsend.at[1], wrecv.at[1], there)
    gain_in = remote(gain_ref, gb.at[other], wsend.at[2], wrecv.at[2], there)
    wq_fwd = remote(wq_theirs, wq_theirs, fsend.at[0], frecv.at[0], beside)
    wo_fwd = remote(wo.at[other, mine_o], wo.at[other, mine_o], fsend.at[1], frecv.at[1], beside)
    wq_fwd_in = remote(wq_mates, wq_mates, fsend.at[0], frecv.at[0], beside)
    wo_fwd_in = remote(wo.at[other, mate_o], wo.at[other, mate_o], fsend.at[1], frecv.at[1], beside)

    def columns(owner):
        return pl.ds(pl.multiple_of(owner * feat, 128), feat)

    def layer_compute(layer, src):
        ag[layer, me] = src[...]

        def norm_half(i, carry):
            rows = pl.ds(pl.multiple_of(i * half, 16), half)
            total = jnp.zeros((half, 1), jnp.float32)
            for owner in range(n_head):
                value = ag[layer, owner, rows, :].astype(jnp.float32)
                total = total + jnp.sum(value * value, axis=-1, keepdims=True)
            scale = lax.rsqrt(total / (feat * n_head) + 1e-05)
            for owner in range(n_head):
                cols = slice(owner * feat, (owner + 1) * feat)
                value = ag[layer, owner, rows, :].astype(jnp.float32)
                normed[rows, cols] = (value * scale * gb[layer, 0:1, cols]).astype(jnp.bfloat16)
            return carry

        lax.fori_loop(0, 2, norm_half, 0)
        if layer == 0:
            wq_local.wait()
            wq_fwd_in.wait_recv()

        def qkv_half(i, carry):
            rows = pl.ds(pl.multiple_of(i * half, 16), half)
            for slot in range(3):
                value = jnp.dot(normed[rows, :], wq[layer, slot],
                                preferred_element_type=jnp.float32)
                if slot == 0:
                    value = value * (HEAD_DIM ** -0.5 * math.log2(math.e))
                if slot < 2:
                    qkv[rows, slot * feat:(slot + 1) * feat] = value.astype(jnp.bfloat16)
                else:
                    for h in range(heads):
                        vx[h, rows, :HEAD_DIM] = value[
                            :, h * HEAD_DIM:(h + 1) * HEAD_DIM].astype(jnp.bfloat16)
            return carry

        lax.fori_loop(0, 2, qkv_half, 0)
        if layer == 0:
            wo_in.wait_recv()
            wo_fwd.start()
            wo_local.wait()
            wo_fwd_in.wait_recv()

        def attend_half(i, carry):
            for sub in range(2):
                offset, count = blocks[sub]
                rows = pl.ds(pl.multiple_of(i * half + offset, 16), count)
                for h in range(heads):
                    q = qkv[rows, h * HEAD_DIM:(h + 1) * HEAD_DIM]
                    k = qkv[:, feat + h * HEAD_DIM:feat + (h + 1) * HEAD_DIM]
                    scores = lax.dot_general(q, k, (((1,), (1,)), ((), ())),
                                             preferred_element_type=jnp.float32)
                    scores = jnp.where(lq_ref[layer, rows, :] == lk_ref[layer], scores, -1e30)
                    top = jnp.max(scores, axis=-1, keepdims=True)
                    expo = jnp.exp2(scores - top).astype(jnp.bfloat16)
                    both = jnp.dot(expo, vx[h], preferred_element_type=jnp.float32)
                    attb[rows, h * HEAD_DIM:(h + 1) * HEAD_DIM] = (
                        both[:, :HEAD_DIM] / both[:, HEAD_DIM:]).astype(jnp.bfloat16)
                block = attb[rows, :]
                for owner in range(n_head):
                    part[owner, rows, :] = jnp.dot(
                        block, wo[layer, :, owner * feat:(owner + 1) * feat],
                        preferred_element_type=jnp.float32)

                @pl.when(me == 0)
                def _(rows=rows, sub=sub):
                    for owner in range(last, 0, -1):
                        sums[layer, owner, rows, :] = part[owner, rows, :].astype(jnp.bfloat16)
                        sum_copy(layer, 0, i * 2 + sub, rows, owner).start()

                @pl.when(me == last)
                def _(rows=rows, sub=sub):
                    for owner in range(last):
                        sums[layer, owner, rows, :] = part[owner, rows, :].astype(jnp.bfloat16)
                        sum_copy(layer, 1, i * 2 + sub, rows, owner).start()
            return carry

        lax.fori_loop(0, 2, attend_half, 0)

    def finish(layer, src, block):
        rows = rows_of(block)
        for far in range(last - 1, -1, -1):
            for way, owner, takes in ((0, me + far, me > 0), (1, me - far, me < last)):
                @pl.when(takes & (owner >= 0) & (owner <= last))
                def _(way=way, owner=owner, far=far):
                    copy = sum_copy(layer, way, block, rows, owner)
                    copy.wait_recv()
                    total = part[owner, rows, :] + sums_in[
                        layer, way, owner, rows, :].astype(jnp.float32)
                    if far:
                        sums[layer, owner, rows, :] = total.astype(jnp.bfloat16)
                        copy.start()
                    else:
                        part[owner, rows, :] = total
        total = src[rows, :].astype(jnp.float32) + part[me, rows, :]
        return rows, total.astype(jnp.bfloat16)

    def sums_sent(layer, block):
        for far in range(1, n_head):
            for way, owner in ((0, me + far), (1, me - far)):
                @pl.when((owner >= 0) & (owner <= last))
                def _(way=way, owner=owner):
                    sum_copy(layer, way, block, rows_of(block), owner).wait_send()

    for hop in range(last - 1):
        for block in range(4):
            gather_step(0, hop, block)
    wq_in.wait_recv()
    wq_fwd.start()
    gain_in.wait_recv()
    for block in range(4):
        gather_step(0, last - 1, block)
    layer_compute(0, x_ref)

    low, high = pl.ds(0, half), pl.ds(half, half)
    rolls = []
    for block in range(2):
        rows, value = finish(0, x_ref, block)
        first_a[rows, :] = value
        roll = remote(first_a.at[rows], cur.at[rows_of(2 + block)],
                      roll_send.at[block], roll_recv.at[block], {"win": left})
        roll.start()
        rolls.append(roll)
    for block in range(2):
        rolls[block].wait_recv()
        gather_start(1, cur, 2 + block)
    for block in range(2):
        _, value = finish(0, x_ref, 2 + block)
        cur[rows_of(block), :] = value
        gather_start(1, cur, block)
        if block < last - 1:
            for late in (2, 3):
                gather_step(1, block, late)
    for late in (2, 3):
        for hop in range(min(2, last - 1), last):
            gather_step(1, hop, late)
    for hop in range(last):
        for block in range(2):
            gather_step(1, hop, block)

    first_out = [
        remote(first_a, out_ref.at[seg, low], o_send.at[0], o_recv.at[0], there),
        remote(cur.at[low], out_ref.at[seg, high], o_send.at[1], o_recv.at[1], there),
    ]
    first_in = [
        remote(first_a, out_ref.at[other, low], o_send.at[0], o_recv.at[0], there),
        remote(cur.at[low], out_ref.at[other, high], o_send.at[1], o_recv.at[1], there),
    ]

    @pl.when(seg == 0)
    def _():
        out_ref[seg, low, :] = first_a[...]
        out_ref[seg, high, :] = cur[low, :]

    @pl.when(seg == 1)
    def _():
        for c in first_out:
            c.start()

    layer_compute(1, cur)

    second_sends, second_recvs = [], []
    for block in range(4):
        rows, value = finish(1, cur, block)
        send = remote(second.at[rows], out_ref.at[seg, rows], o_send.at[2 + block],
                      o_recv.at[2 + block], there)
        second_sends.append(send)
        second_recvs.append(remote(second.at[rows], out_ref.at[other, rows],
                                   o_send.at[2 + block], o_recv.at[2 + block], there))
        second[rows, :] = value

        @pl.when(seg == 0)
        def _(send=send):
            send.start()

        @pl.when(seg == 1)
        def _(rows=rows):
            out_ref[seg, rows, :] = second[rows, :]

    for layer, src in ((0, x_ref), (1, cur)):
        for block in range(4):
            gather_sent(layer, src, block)
            sums_sent(layer, block)
    for c in (gain_out, wq_out, wo_out, wq_fwd, wo_fwd, *rolls):
        c.wait_send()

    @pl.when(seg == 0)
    def _():
        for c in first_in:
            c.wait_recv()
        for c in second_sends:
            c.wait_send()

    @pl.when(seg == 1)
    def _():
        for c in first_out:
            c.wait_send()
        for c in second_recvs:
            c.wait_recv()


def to_halves(grid, half, fill):
    rows, cols, features = grid.shape
    split = grid.reshape(rows, 2, cols // 2, features).transpose(1, 0, 2, 3)
    split = split.reshape(2, rows * (cols // 2), features)
    split = jnp.pad(split, ((0, 0), (0, half - split.shape[1]), (0, 0)), constant_values=fill)
    return split.reshape(2 * half, features)


def body(n_head, n_win, inputs, gains, qkv_weight, out_weight, labels):
    seg = lax.axis_index("segment")
    micro, win_rows, win_cols, feat = inputs.shape
    cells = win_rows * (win_cols // 2)
    half = pad16(cells)
    tokens = 2 * half
    model = feat * n_head
    heads = feat // HEAD_DIM
    x = lax.dynamic_index_in_dim(inputs, seg, 0, keepdims=False)
    x = to_halves(x, half, 0)
    grid = labels[:, :, None]
    keys = jnp.stack([to_halves(jnp.zeros_like(grid), half, -1), to_halves(grid, half, -1)])
    queries = jnp.maximum(keys, 0)
    keys = keys.reshape(LAYERS, 1, tokens)
    gain_rows = jnp.broadcast_to(gains, (8, model))
    wq = qkv_weight[0].transpose(1, 0, 2)
    wo = out_weight[0]
    bf16, f32 = jnp.bfloat16, jnp.float32
    others = n_head - 1
    dma = pltpu.SemaphoreType.DMA
    vmem = pl.BlockSpec(memory_space=pltpu.VMEM)
    hbm = pl.BlockSpec(memory_space=pl.ANY)
    out = pl.pallas_call(
        functools.partial(two_layers, n_head, n_win, half),
        out_shape=jax.ShapeDtypeStruct((micro, tokens, feat), bf16),
        in_specs=[vmem, vmem, vmem, vmem, hbm, hbm],
        out_specs=vmem,
        scratch_shapes=[
            pltpu.VMEM((LAYERS, 3, model, feat), bf16),
            pltpu.VMEM((LAYERS, feat, model), bf16),
            pltpu.VMEM((LAYERS, 8, model), f32),
            pltpu.VMEM((LAYERS, n_head, tokens, feat), bf16),
            pltpu.VMEM((tokens, model), bf16),
            pltpu.VMEM((tokens, 2 * feat), bf16),
            pltpu.VMEM((heads, tokens, 2 * HEAD_DIM), bf16),
            pltpu.VMEM((tokens, feat), bf16),
            pltpu.VMEM((n_head, tokens, feat), f32),
            pltpu.VMEM((LAYERS, n_head, tokens, feat), bf16),
            pltpu.VMEM((LAYERS, 2, n_head, tokens, feat), bf16),
            pltpu.VMEM((tokens, feat), bf16),
            pltpu.VMEM((half, feat), bf16),
            pltpu.VMEM((tokens, feat), bf16),
            dma((2,)), dma((3,)), dma((3,)), dma((2,)), dma((2,)),
            dma((LAYERS, 2, others, 4)), dma((LAYERS, 2, others, 4)),
            dma((LAYERS, 2, 4, n_head)), dma((LAYERS, 2, 4, n_head)),
            dma((2,)), dma((2,)), dma((6,)), dma((6,)),
        ],
        compiler_params=pltpu.CompilerParams(
            collective_id=0, has_side_effects=True, vmem_limit_bytes=58 * 2 ** 20),
    )(x, gain_rows, queries, keys, wq, wo)
    out = out.reshape(micro, 2, half, feat)[:, :, :cells]
    out = out.reshape(micro, 2, win_rows, win_cols // 2, feat).transpose(0, 2, 1, 3, 4)
    return out.reshape(1, micro, win_rows, win_cols, feat)


def solution(mesh):
    in_specs = (
        P(None, None, "win", "head"),
        P("segment", None),
        P("segment", None, None, "head"),
        P("segment", "head", None),
        P(None, "win"),
    )
    out_specs = P("segment", None, None, "win", "head")
    run = functools.partial(body, mesh.shape["head"], mesh.shape["win"])
    return jax.shard_map(run, mesh=mesh, in_specs=in_specs, out_specs=out_specs, check_vma=False)
```

```python
import functools
import math

import jax
import jax.numpy as jnp
from jax import lax
from jax.experimental import pallas as pl
from jax.experimental.pallas import tpu as pltpu
from jax.sharding import PartitionSpec as P

HEAD_DIM = 128
WIN_SIDE = 30
MESH = pl.DeviceIdType.MESH
LAYERS = 2


def pad16(n):
    return -(-n // 16) * 16


def remote(src, dst, send, recv, device):
    return pltpu.make_async_remote_copy(
        src_ref=src, dst_ref=dst, send_sem=send, recv_sem=recv,
        device_id=device, device_id_type=MESH,
    )


def two_layers(
    n_head, n_win, half,
    x_ref, gain_ref, lq_ref, lk_ref, wq_hbm, wo_hbm,
    out_ref,
    wq, wo, gb, ag, normed, qkv, vx, attb, part, sums, sums_in, cur, first_a, second,
    loc_sem, wsend, wrecv, fsend, frecv, ag_send, ag_recv, rs_send, rs_recv,
    roll_send, roll_recv, o_send, o_recv,
):
    seg = lax.axis_index("segment")
    win = lax.axis_index("win")
    me = lax.axis_index("head")
    last = n_head - 1
    other = 1 - seg
    core = lax.rem(win, 2)
    mate = win + 1 - 2 * core
    left = lax.rem(win + n_win - 1, n_win)
    right = lax.rem(win + 1, n_win)
    tokens, feat = x_ref.shape
    heads = feat // HEAD_DIM
    first_rows = pad16(half // 2)
    blocks = ((0, first_rows), (first_rows, half - first_rows),
              (half, first_rows), (half + first_rows, half - first_rows))
    up, down = {"head": me + 1}, {"head": me - 1}
    there, beside = {"segment": other}, {"win": mate}

    wq_local = pltpu.make_async_copy(wq_hbm, wq.at[seg], loc_sem.at[0])
    wo_local = pltpu.make_async_copy(wo_hbm, wo.at[seg], loc_sem.at[1])
    wq_local.start()
    wo_local.start()

    barrier = pltpu.get_barrier_semaphore()

    @pl.when(me < last)
    def _():
        pl.semaphore_signal(barrier, inc=1, device_id=up, device_id_type=MESH)

    @pl.when(me > 0)
    def _():
        pl.semaphore_signal(barrier, inc=1, device_id=down, device_id_type=MESH)

    pl.semaphore_signal(barrier, inc=1, device_id=there, device_id_type=MESH)
    for w in (mate, left, right):
        pl.semaphore_signal(barrier, inc=1, device_id={"win": w}, device_id_type=MESH)

    @pl.when((me > 0) & (me < last))
    def _():
        pl.semaphore_wait(barrier, 6)

    @pl.when((me == 0) | (me == last))
    def _():
        pl.semaphore_wait(barrier, 5)

    def rows_of(block):
        return pl.ds(blocks[block][0], blocks[block][1])

    def ag_copy(layer, way, hop, block, owner, src):
        rows = rows_of(block)
        source = ag.at[layer, owner, rows] if src is None else src.at[rows]
        return remote(source, ag.at[layer, owner, rows], ag_send.at[layer, way, hop, block],
                      ag_recv.at[layer, way, hop, block], up if way == 0 else down)

    def gather_start(layer, src, block):
        @pl.when(me < last)
        def _():
            ag_copy(layer, 0, 0, block, me, src).start()

        @pl.when(me > 0)
        def _():
            ag_copy(layer, 1, 0, block, me, src).start()

    def gather_step(layer, hop, block):
        behind, ahead = me - 1 - hop, me + 1 + hop

        @pl.when(behind >= 0)
        def _():
            ag_copy(layer, 0, hop, block, behind, None).wait_recv()
            if hop + 1 < last:
                @pl.when(me < last)
                def _():
                    ag_copy(layer, 0, hop + 1, block, behind, None).start()

        @pl.when(ahead <= last)
        def _():
            ag_copy(layer, 1, hop, block, ahead, None).wait_recv()
            if hop + 1 < last:
                @pl.when(me > 0)
                def _():
                    ag_copy(layer, 1, hop + 1, block, ahead, None).start()

    def gather_sent(layer, src, block):
        for hop in range(last):
            @pl.when((me - hop >= 0) & (me < last))
            def _(hop=hop):
                ag_copy(layer, 0, hop, block, me - hop, None if hop else src).wait_send()

            @pl.when((me + hop <= last) & (me > 0))
            def _(hop=hop):
                ag_copy(layer, 1, hop, block, me + hop, None if hop else src).wait_send()

    def sum_copy(layer, way, block, rows, owner):
        return remote(sums.at[layer, owner, rows], sums_in.at[layer, way, owner, rows],
                      rs_send.at[layer, way, block, owner], rs_recv.at[layer, way, block, owner],
                      up if way == 0 else down)

    q_rows, o_rows = wq_hbm.shape[1] // 2, wo_hbm.shape[0] // 2
    mine_q = pl.ds(pl.multiple_of(core * q_rows, 16), q_rows)
    mine_o = pl.ds(pl.multiple_of(core * o_rows, 16), o_rows)
    mate_q = pl.ds(pl.multiple_of((1 - core) * q_rows, 16), q_rows)
    mate_o = pl.ds(pl.multiple_of((1 - core) * o_rows, 16), o_rows)
    every = pl.ds(0, 3)

    for block in range(4):
        gather_start(0, x_ref, block)
    gain_out = remote(gain_ref, gb.at[seg], wsend.at[2], wrecv.at[2], there)
    wq_out = remote(wq_hbm.at[every, mine_q], wq.at[seg, every, mine_q],
                    wsend.at[0], wrecv.at[0], there)
    wo_out = remote(wo_hbm.at[mine_o], wo.at[seg, mine_o], wsend.at[1], wrecv.at[1], there)
    gain_out.start()
    wq_out.start()
    gb[seg] = gain_ref[...]
    for h in range(heads):
        vx[h, :, HEAD_DIM:] = jnp.ones((tokens, HEAD_DIM), jnp.bfloat16)

    wq_theirs, wq_mates = wq.at[other, every, mine_q], wq.at[other, every, mate_q]
    wq_in = remote(wq_hbm.at[every, mine_q], wq_theirs, wsend.at[0], wrecv.at[0], there)
    wo_in = remote(wo_hbm.at[mine_o], wo.at[other, mine_o], wsend.at[1], wrecv.at[1], there)
    gain_in = remote(gain_ref, gb.at[other], wsend.at[2], wrecv.at[2], there)
    wq_fwd = remote(wq_theirs, wq_theirs, fsend.at[0], frecv.at[0], beside)
    wo_fwd = remote(wo.at[other, mine_o], wo.at[other, mine_o], fsend.at[1], frecv.at[1], beside)
    wq_fwd_in = remote(wq_mates, wq_mates, fsend.at[0], frecv.at[0], beside)
    wo_fwd_in = remote(wo.at[other, mate_o], wo.at[other, mate_o], fsend.at[1], frecv.at[1], beside)

    def columns(owner):
        return pl.ds(pl.multiple_of(owner * feat, 128), feat)

    def prepare(layer, src, begin, end):
        def norm_half(i, carry):
            rows = pl.ds(pl.multiple_of(i * half, 16), half)
            ag[layer, me, rows, :] = src[rows, :]
            total = jnp.zeros((half, 1), jnp.float32)
            for owner in range(n_head):
                value = ag[layer, owner, rows, :].astype(jnp.float32)
                total = total + jnp.sum(value * value, axis=-1, keepdims=True)
            scale = lax.rsqrt(total / (feat * n_head) + 1e-05)
            for owner in range(n_head):
                cols = slice(owner * feat, (owner + 1) * feat)
                value = ag[layer, owner, rows, :].astype(jnp.float32)
                normed[rows, cols] = (value * scale * gb[layer, 0:1, cols]).astype(jnp.bfloat16)
            return carry

        lax.fori_loop(begin, end, norm_half, 0)
        if layer == 0:
            wq_local.wait()
            wq_fwd_in.wait_recv()

        def qkv_half(i, carry):
            rows = pl.ds(pl.multiple_of(i * half, 16), half)
            for slot in range(3):
                value = jnp.dot(normed[rows, :], wq[layer, slot],
                                preferred_element_type=jnp.float32)
                if slot == 0:
                    value = value * (HEAD_DIM ** -0.5 * math.log2(math.e))
                if slot < 2:
                    qkv[rows, slot * feat:(slot + 1) * feat] = value.astype(jnp.bfloat16)
                else:
                    for h in range(heads):
                        vx[h, rows, :HEAD_DIM] = value[
                            :, h * HEAD_DIM:(h + 1) * HEAD_DIM].astype(jnp.bfloat16)
            return carry

        lax.fori_loop(begin, end, qkv_half, 0)

    def attend(layer):
        if layer == 0:
            wo_in.wait_recv()
            wo_fwd.start()
            wo_local.wait()
            wo_fwd_in.wait_recv()

        def attend_half(i, carry):
            for sub in range(2):
                offset, count = blocks[sub]
                rows = pl.ds(pl.multiple_of(i * half + offset, 16), count)
                for h in range(heads):
                    q = qkv[rows, h * HEAD_DIM:(h + 1) * HEAD_DIM]
                    k = qkv[:, feat + h * HEAD_DIM:feat + (h + 1) * HEAD_DIM]
                    scores = lax.dot_general(q, k, (((1,), (1,)), ((), ())),
                                             preferred_element_type=jnp.float32)
                    scores = jnp.where(lq_ref[layer, rows, :] == lk_ref[layer], scores, -1e30)
                    top = jnp.max(scores, axis=-1, keepdims=True)
                    expo = jnp.exp2(scores - top).astype(jnp.bfloat16)
                    both = jnp.dot(expo, vx[h], preferred_element_type=jnp.float32)
                    attb[rows, h * HEAD_DIM:(h + 1) * HEAD_DIM] = (
                        both[:, :HEAD_DIM] / both[:, HEAD_DIM:]).astype(jnp.bfloat16)
                block = attb[rows, :]
                for owner in range(n_head):
                    part[owner, rows, :] = jnp.dot(
                        block, wo[layer, :, owner * feat:(owner + 1) * feat],
                        preferred_element_type=jnp.float32)

                @pl.when(me == 0)
                def _(rows=rows, sub=sub):
                    for owner in range(last, 0, -1):
                        sums[layer, owner, rows, :] = part[owner, rows, :].astype(jnp.bfloat16)
                        sum_copy(layer, 0, i * 2 + sub, rows, owner).start()

                @pl.when(me == last)
                def _(rows=rows, sub=sub):
                    for owner in range(last):
                        sums[layer, owner, rows, :] = part[owner, rows, :].astype(jnp.bfloat16)
                        sum_copy(layer, 1, i * 2 + sub, rows, owner).start()
            return carry

        lax.fori_loop(0, 2, attend_half, 0)

    def finish(layer, src, block):
        rows = rows_of(block)
        for far in range(last - 1, -1, -1):
            for way, owner, takes in ((0, me + far, me > 0), (1, me - far, me < last)):
                @pl.when(takes & (owner >= 0) & (owner <= last))
                def _(way=way, owner=owner, far=far):
                    copy = sum_copy(layer, way, block, rows, owner)
                    copy.wait_recv()
                    total = part[owner, rows, :] + sums_in[
                        layer, way, owner, rows, :].astype(jnp.float32)
                    if far:
                        sums[layer, owner, rows, :] = total.astype(jnp.bfloat16)
                        copy.start()
                    else:
                        part[owner, rows, :] = total
        total = src[rows, :].astype(jnp.float32) + part[me, rows, :]
        return rows, total.astype(jnp.bfloat16)

    def sums_sent(layer, block):
        for far in range(1, n_head):
            for way, owner in ((0, me + far), (1, me - far)):
                @pl.when((owner >= 0) & (owner <= last))
                def _(way=way, owner=owner):
                    sum_copy(layer, way, block, rows_of(block), owner).wait_send()

    for hop in range(last - 1):
        for block in range(4):
            gather_step(0, hop, block)
    wq_in.wait_recv()
    wq_fwd.start()
    wo_out.start()
    gain_in.wait_recv()
    for block in range(4):
        gather_step(0, last - 1, block)
    prepare(0, x_ref, 0, 2)
    attend(0)

    low, high = pl.ds(0, half), pl.ds(half, half)
    rolls = []
    for block in range(2):
        rows, value = finish(0, x_ref, block)
        first_a[rows, :] = value
        roll = remote(first_a.at[rows], cur.at[rows_of(2 + block)],
                      roll_send.at[block], roll_recv.at[block], {"win": left})
        roll.start()
        rolls.append(roll)
    for block in range(2):
        rolls[block].wait_recv()
        gather_start(1, cur, 2 + block)
    for block in range(2):
        _, value = finish(0, x_ref, 2 + block)
        cur[rows_of(block), :] = value
        gather_start(1, cur, block)
        if block < last - 1:
            for late in (2, 3):
                gather_step(1, block, late)
    for late in (2, 3):
        for hop in range(min(2, last - 1), last):
            gather_step(1, hop, late)
    for hop in range(last):
        for block in range(2):
            gather_step(1, hop, block)
        if hop == 0:
            prepare(1, cur, 1, 2)
    prepare(1, cur, 0, 1)

    first_out = [
        remote(first_a, out_ref.at[seg, low], o_send.at[0], o_recv.at[0], there),
        remote(cur.at[low], out_ref.at[seg, high], o_send.at[1], o_recv.at[1], there),
    ]
    first_in = [
        remote(first_a, out_ref.at[other, low], o_send.at[0], o_recv.at[0], there),
        remote(cur.at[low], out_ref.at[other, high], o_send.at[1], o_recv.at[1], there),
    ]

    @pl.when(seg == 0)
    def _():
        out_ref[seg, low, :] = first_a[...]
        out_ref[seg, high, :] = cur[low, :]

    @pl.when(seg == 1)
    def _():
        for c in first_out:
            c.start()

    attend(1)

    second_sends, second_recvs = [], []
    for block in range(4):
        rows, value = finish(1, cur, block)
        send = remote(second.at[rows], out_ref.at[seg, rows], o_send.at[2 + block],
                      o_recv.at[2 + block], there)
        second_sends.append(send)
        second_recvs.append(remote(second.at[rows], out_ref.at[other, rows],
                                   o_send.at[2 + block], o_recv.at[2 + block], there))
        second[rows, :] = value

        @pl.when(seg == 0)
        def _(send=send):
            send.start()

        @pl.when(seg == 1)
        def _(rows=rows):
            out_ref[seg, rows, :] = second[rows, :]

    for layer, src in ((0, x_ref), (1, cur)):
        for block in range(4):
            gather_sent(layer, src, block)
            sums_sent(layer, block)
    for c in (gain_out, wq_out, wo_out, wq_fwd, wo_fwd, *rolls):
        c.wait_send()

    @pl.when(seg == 0)
    def _():
        for c in first_in:
            c.wait_recv()
        for c in second_sends:
            c.wait_send()

    @pl.when(seg == 1)
    def _():
        for c in first_out:
            c.wait_send()
        for c in second_recvs:
            c.wait_recv()


def to_halves(grid, half, fill):
    rows, cols, features = grid.shape
    split = grid.reshape(rows, 2, cols // 2, features).transpose(1, 0, 2, 3)
    split = split.reshape(2, rows * (cols // 2), features)
    split = jnp.pad(split, ((0, 0), (0, half - split.shape[1]), (0, 0)), constant_values=fill)
    return split.reshape(2 * half, features)


def body(n_head, n_win, inputs, gains, qkv_weight, out_weight, labels):
    seg = lax.axis_index("segment")
    micro, win_rows, win_cols, feat = inputs.shape
    cells = win_rows * (win_cols // 2)
    half = pad16(cells)
    tokens = 2 * half
    model = feat * n_head
    heads = feat // HEAD_DIM
    x = lax.dynamic_index_in_dim(inputs, seg, 0, keepdims=False)
    x = to_halves(x, half, 0)
    grid = labels[:, :, None]
    keys = jnp.stack([to_halves(jnp.zeros_like(grid), half, -1), to_halves(grid, half, -1)])
    queries = jnp.maximum(keys, 0)
    keys = keys.reshape(LAYERS, 1, tokens)
    gain_rows = jnp.broadcast_to(gains, (8, model))
    wq = qkv_weight[0].transpose(1, 0, 2)
    wo = out_weight[0]
    bf16, f32 = jnp.bfloat16, jnp.float32
    others = n_head - 1
    dma = pltpu.SemaphoreType.DMA
    vmem = pl.BlockSpec(memory_space=pltpu.VMEM)
    hbm = pl.BlockSpec(memory_space=pl.ANY)
    out = pl.pallas_call(
        functools.partial(two_layers, n_head, n_win, half),
        out_shape=jax.ShapeDtypeStruct((micro, tokens, feat), bf16),
        in_specs=[vmem, vmem, vmem, vmem, hbm, hbm],
        out_specs=vmem,
        scratch_shapes=[
            pltpu.VMEM((LAYERS, 3, model, feat), bf16),
            pltpu.VMEM((LAYERS, feat, model), bf16),
            pltpu.VMEM((LAYERS, 8, model), f32),
            pltpu.VMEM((LAYERS, n_head, tokens, feat), bf16),
            pltpu.VMEM((tokens, model), bf16),
            pltpu.VMEM((tokens, 2 * feat), bf16),
            pltpu.VMEM((heads, tokens, 2 * HEAD_DIM), bf16),
            pltpu.VMEM((tokens, feat), bf16),
            pltpu.VMEM((n_head, tokens, feat), f32),
            pltpu.VMEM((LAYERS, n_head, tokens, feat), bf16),
            pltpu.VMEM((LAYERS, 2, n_head, tokens, feat), bf16),
            pltpu.VMEM((tokens, feat), bf16),
            pltpu.VMEM((half, feat), bf16),
            pltpu.VMEM((tokens, feat), bf16),
            dma((2,)), dma((3,)), dma((3,)), dma((2,)), dma((2,)),
            dma((LAYERS, 2, others, 4)), dma((LAYERS, 2, others, 4)),
            dma((LAYERS, 2, 4, n_head)), dma((LAYERS, 2, 4, n_head)),
            dma((2,)), dma((2,)), dma((6,)), dma((6,)),
        ],
        compiler_params=pltpu.CompilerParams(
            collective_id=0, has_side_effects=True, vmem_limit_bytes=58 * 2 ** 20),
    )(x, gain_rows, queries, keys, wq, wo)
    out = out.reshape(micro, 2, half, feat)[:, :, :cells]
    out = out.reshape(micro, 2, win_rows, win_cols // 2, feat).transpose(0, 2, 1, 3, 4)
    return out.reshape(1, micro, win_rows, win_cols, feat)


def solution(mesh):
    in_specs = (
        P(None, None, "win", "head"),
        P("segment", None),
        P("segment", None, None, "head"),
        P("segment", "head", None),
        P(None, "win"),
    )
    out_specs = P("segment", None, None, "win", "head")
    run = functools.partial(body, mesh.shape["head"], mesh.shape["win"])
    return jax.shard_map(run, mesh=mesh, in_specs=in_specs, out_specs=out_specs, check_vma=False)
```
